512 devices in a mesh: rep: 16 (over y, x_hi), fsdp: 32 (over z, x_lo, core).
Axes of the slice: x: 4 (x_hi: 2, x_lo: 2; x = x_hi * 2 + x_lo), y: 8, z: 8, core: 2. Of those that a mesh axis runs over, the one named last changes fastest.
Arguments:
- gradient: bfloat16 [16, 5120, 4096], P('rep', 'fsdp'), may hold values from -4 to 4
- momentum: bfloat16 [16, 5120, 4096], P('rep', 'fsdp'), may hold values from -2 to 2
- pseudo_gradient: bfloat16 [16, 5120, 1024], P('rep', 'fsdp'), may hold values from -8 to 8
- outer_momentum: bfloat16 [5120, 1024], P('fsdp'), may hold values from -6 to 6
Outputs:
- update: bfloat16 [16, 5120, 4096], P('rep', 'fsdp')
- renewed: bfloat16 [5120, 1024], P('fsdp')
The draws below stay inside these ranges and needn't reach their ends.
All inputs are finite; a program needn't handle non-finite values.
Results may differ from the reference program's by a relative error of at most 0.014.
Values may be sent and summed in bfloat16 or wider, within the bound.
A program may use at most 64 MiB of HBM per device.

```python
import math
import jax
import jax.numpy as jnp
from jax import lax

D = 5120
KV_ROWS = 1024
HD = 128
ITERS = 5
HEADS = 32
REPLICAS = 16


def shared_scales(key):
    row_scale = jnp.exp(jax.random.uniform(jax.random.fold_in(key, 101), (D, 1), jnp.float32, 0.0, math.log(10.0)))
    column_scale = jnp.exp(jax.random.uniform(jax.random.fold_in(key, 102), (1, HEADS * HD), jnp.float32, 0.0, math.log(10.0)))
    return row_scale * column_scale


def varied_values_keyed(scales_key, noise_key, factor):
    scales = shared_scales(scales_key)
    fluctuation = jnp.clip(jax.random.normal(noise_key, (REPLICAS, D, HEADS * HD), jnp.float32), -4.0, 4.0)
    return jnp.clip(0.01 * factor * fluctuation * scales, -4.0 * factor, 4.0 * factor)


def draw_gradient(key, part):
    scales_key = key
    key = jax.random.fold_in(key, 7)
    values = varied_values_keyed(scales_key, key, 1.0)
    return values.astype(jnp.bfloat16)


def draw_momentum(key, part):
    scales_key = key
    key = jax.random.fold_in(key, 8)
    values = varied_values_keyed(scales_key, key, 0.5)
    return values.astype(jnp.bfloat16)


def shard_levels(stream_key, extent, cuts, smallest, high):
    def one(axis_at, parts):
        heights = jax.random.uniform(jax.random.fold_in(jax.random.fold_in(stream_key, 6), axis_at), (parts,), jnp.float32, smallest / len(cuts), high / len(cuts))
        return jnp.repeat(jnp.exp(heights), extent[axis_at] // parts).reshape((-1,) + (1,) * (len(extent) - axis_at - 1))

    gain = one(*cuts[0])
    for cut in cuts[1:]:
        gain = gain * one(*cut)
    return gain


def normal_values(own_key, shape, spread, limit, shards=(), held_as=jnp.bfloat16):
    factor_of = shard_levels(own_key, shape, shards, -0.22, 0.18) if shards else 1.0
    entries = jax.random.normal(own_key, shape, jnp.float32) * spread * factor_of
    return jnp.minimum(jnp.maximum(entries, -limit), limit).astype(held_as)


def setup_inputs(seed: int = 0) -> dict:
    streams_of = jax.random.split(jax.random.key(seed), 5)
    gradient = draw_gradient(jax.random.fold_in(streams_of[4], 71), 0)
    momentum = draw_momentum(jax.random.fold_in(streams_of[4], 71), 0)
    pseudo_gradient = normal_values(streams_of[2], (REPLICAS, D, KV_ROWS), 2.0, 8.0, ((0, 16), (1, 32)))
    outer_momentum = normal_values(streams_of[3], (D, KV_ROWS), 1.0, 6.0, ((0, 32),))
    return {"gradient": gradient, "momentum": momentum, "pseudo_gradient": pseudo_gradient, "outer_momentum": outer_momentum}


quint_a = 3.4445
quint_b = -4.775
quint_c = 2.0315
inner_beta = 0.95
outer_beta = 0.9
norm_eps = 1e-07
highest = lax.Precision.HIGHEST

def orthogonal(head_block):
    matrix = head_block.astype(jnp.float32)
    matrix = matrix / (jnp.sqrt(jnp.sum(matrix * matrix)) + norm_eps)
    for sweep_index in range(ITERS):
        gram_matrix = jnp.dot(matrix.T, matrix, precision=highest, preferred_element_type=jnp.float32)
        polynomial = quint_b * gram_matrix + quint_c * jnp.dot(gram_matrix, gram_matrix, precision=highest, preferred_element_type=jnp.float32)
        matrix = quint_a * matrix + jnp.dot(matrix, polynomial, precision=highest, preferred_element_type=jnp.float32)
    return (math.sqrt(D) * matrix).astype(jnp.bfloat16)

def reference(gradient, momentum, pseudo_gradient, outer_momentum):
    grad_wide = gradient.astype(jnp.float32)
    velocity = inner_beta * momentum.astype(jnp.float32) + grad_wide
    nesterov = (grad_wide + inner_beta * velocity).astype(jnp.bfloat16)
    blocks = nesterov.reshape(REPLICAS, D, HEADS, HD).transpose(0, 2, 1, 3).reshape(REPLICAS * HEADS, D, HD)
    update = lax.map(orthogonal, blocks).reshape(REPLICAS, HEADS, D, HD).transpose(0, 2, 1, 3).reshape(REPLICAS, D, HEADS * HD)
    summed = lax.optimization_barrier(jnp.sum(pseudo_gradient.astype(jnp.float32), axis=0))
    renewed = (outer_beta * outer_momentum.astype(jnp.float32) + summed / REPLICAS).astype(jnp.bfloat16)
    return (update, renewed)
```

```python
import functools
import math

import jax
import jax.numpy as jnp
from jax import lax
from jax.experimental import pallas as pl
from jax.experimental.pallas import tpu as pltpu
from jax.sharding import PartitionSpec as P

HD = 128
HALF = HD // 2
PACK = HALF + 8
ITERS = 5

quint_a = 3.4445
quint_b = -4.775
quint_c = 2.0315
inner_beta = 0.95
outer_beta = 0.9
norm_eps = 1e-07
highest = lax.Precision.HIGHEST
f32 = jnp.float32
bf16 = jnp.bfloat16


def far_first(n):
    return sorted(range(n), key=lambda d: (-min(d, n - d), d))


def iota(axis, rows=HALF):
    return lax.broadcasted_iota(jnp.int32, (rows, HD), axis)


def masks():
    row, lane = iota(0), iota(1)
    upper = ((lane < HALF) & (lane >= row)) | ((lane >= HALF) & (lane - HALF < row))
    return upper, lane == row + HALF


def pack(full, upper, cross):
    top, low = full[:HALF], full[HALF:]
    diagonal = jnp.sum(jnp.where(cross, top, 0.0), axis=0, keepdims=True)
    return jnp.where(upper, top, low), jnp.broadcast_to(diagonal, (PACK - HALF, HD))


def spread(ref, upper, cross):
    body = ref[:HALF, :]
    top = jnp.where(upper, body, jnp.where(cross, ref[HALF : HALF + 1, :], 0.0))
    return jnp.concatenate([top, jnp.where(upper, 0.0, body)], axis=0)


def exact_dot(a, b):
    return jnp.dot(a, b, precision=highest, preferred_element_type=f32)


def kernel(
    nz, ny, grad, mom, pseudo, outer, update, renewed,
    gbuf, mbuf, oth, both, xs, xr, own, zr, mine, mz, mx, ms, out,
    yr, pself, pout, half_own, half_in, fresh,
    in_sem, core_sem, x_sem, z_sem, mz_sem, mx_sem, ms_sem, out_sem, y_sem, h_sem, r_sem, p_sem,
):
    rep, fsdp = lax.axis_index("rep"), lax.axis_index("fsdp")
    core, xl, z = fsdp % 2, (fsdp // 2) % 2, fsdp // 4
    xh, y = rep % 2, rep // 2
    rows, cols = oth.shape
    heads = cols // HD
    z_order, y_order = far_first(nz), far_first(ny)

    def at_z(d):
        return {"fsdp": (lax.rem(z + d, nz) * 2 + xl) * 2 + core}

    def at_y(d):
        return {"rep": lax.rem(y + d, ny) * 2 + xh}

    x_peer = {"fsdp": (z * 2 + (1 - xl)) * 2 + core}
    sibling = {"fsdp": (z * 2 + xl) * 2 + (1 - core)}
    h_peer = {"rep": y * 2 + (1 - xh)}
    z_peers = [at_z(d) for d in range(1, nz)]
    y_peers = [at_y(d) for d in range(1, ny)]
    everyone = [sibling, x_peer, h_peer] + z_peers + y_peers

    barrier = pltpu.get_barrier_semaphore()
    for peer in everyone:
        pl.semaphore_signal(barrier, inc=1, device_id=peer, device_id_type=pl.DeviceIdType.MESH)

    def remote(src, dst, sems, i, peer):
        return pltpu.make_async_remote_copy(
            src_ref=src, dst_ref=dst, send_sem=sems.at[0, i], recv_sem=sems.at[1, i],
            device_id=peer, device_id_type=pl.DeviceIdType.MESH,
        )

    chunks = gbuf.shape[0] // 2
    width = gbuf.shape[2]
    loads = []
    for part in range(2):
        base = (1 - core if part == 0 else core) * cols
        for q in range(chunks):
            j = part * chunks + q
            where = pl.ds(pl.multiple_of(base + q * width, HD), width)
            pair = (
                pltpu.make_async_copy(grad.at[0, :, where], gbuf.at[j], in_sem.at[0, j]),
                pltpu.make_async_copy(mom.at[0, :, where], mbuf.at[j], in_sem.at[1, j]),
            )
            pair[0].start()
            pair[1].start()
            loads.append(pair)
    y_cols = pl.ds(pl.multiple_of(y * HD, HD), HD)
    self_copies = (
        pltpu.make_async_copy(pseudo.at[0, :, y_cols], pself, p_sem.at[0]),
        pltpu.make_async_copy(outer.at[:, y_cols], pout, p_sem.at[1]),
    )
    for c in self_copies:
        c.start()

    def nesterov(j):
        for c in loads[j]:
            c.wait()
        g = gbuf[j].astype(f32)
        return (g + inner_beta * (inner_beta * mbuf[j].astype(f32) + g)).astype(bf16)

    sends = []
    core_copies = []
    for q in range(chunks):
        here = pl.ds(q * width, width)
        oth[:, here] = nesterov(q)
        if q == 0:
            pl.semaphore_wait(barrier, len(everyone))
        c = remote(oth.at[:, here], both.at[pl.ds(rows, rows), here], core_sem, q, sibling)
        c.start()
        core_copies.append(c)
    y_copies = {}
    for i, d in enumerate(y_order):
        if d:
            there = pl.ds(pl.multiple_of(lax.rem(y + d, ny) * HD, HD), HD)
            c = remote(pseudo.at[0, :, there], yr.at[i], y_sem, i, at_y(d))
            c.start()
            y_copies[i] = c
    for q in range(chunks):
        both[:rows, pl.ds(q * width, width)] = nesterov(chunks + q)
    for c in core_copies:
        c.wait_recv()

    upper, cross = masks()

    def gram(xo, d):
        at = pl.multiple_of((xo * nz + lax.rem(z + d, nz)) * HD, HD)
        block = both[:, pl.ds(at, HD)]
        full = lax.dot_general(block, block, (((0,), (0,)), ((), ())), preferred_element_type=f32)
        return pack(full, upper, cross)

    x_copies = []
    for i, d in enumerate(z_order):
        body, tail = gram(1 - xl, d)
        xs[i, :HALF, :] = body
        xs[i, HALF:, :] = tail
        c = remote(xs.at[i], xr.at[i], x_sem, i, x_peer)
        c.start()
        x_copies.append(c)
    for i, d in enumerate(z_order):
        body, tail = gram(xl, d)
        own[i, :HALF, :] = body
        own[i, HALF:, :] = tail
    z_copies = {}
    for i, d in enumerate(z_order):
        x_copies[i].wait_recv()
        own[i] = own[i] + xr[i]
        if d:
            c = remote(own.at[i], zr.at[i], z_sem, i, at_z(d))
            c.start()
            z_copies[i] = c

    for c in self_copies:
        c.wait()
    summed = pself[...].astype(f32)
    for i, c in y_copies.items():
        c.wait_recv()
        summed = summed + yr[i].astype(f32)
    half_own[...] = summed.astype(bf16)
    h_copy = remote(half_own, half_in, h_sem, 0, h_peer)
    h_copy.start()

    last = z_order.index(0)
    for i, c in z_copies.items():
        c.wait_recv()
        own[last] = own[last] + zr[i]
    eye = iota(0, HD) == iota(1, HD)
    tri = spread(own.at[last], upper, cross)
    tri = jnp.where(eye, 0.5 * tri, tri)
    matrix = tri + tri.T
    square = 2.0 * jnp.sum(jnp.where(eye, tri, 0.0), keepdims=True)
    scale = 1.0 / (jnp.sqrt(square) + norm_eps)
    matrix = matrix * scale * scale
    ident = jnp.where(eye, quint_a, 0.0)
    product = None
    for sweep in range(ITERS):
        squared = exact_dot(matrix, matrix)
        poly = ident + quint_b * matrix + quint_c * squared
        product = poly if product is None else exact_dot(product, poly)
        if sweep < ITERS - 1:
            matrix = exact_dot(exact_dot(poly, matrix), poly)
    product = product * (scale * math.sqrt(rows * lax.axis_size("fsdp")))
    body, tail = pack(jnp.where(eye, 0.5 * product, product), upper, cross)
    mz[last, :HALF, :] = body
    mz[last, HALF:, :] = tail
    m_copies = {}
    for i, d in enumerate(z_order):
        if d:
            c = remote(mz.at[last], mz.at[i], mz_sem, i, at_z(d))
            c.start()
            m_copies[i] = c

    h_copy.wait_recv()
    total = half_own[...].astype(f32) + half_in[...].astype(f32)
    fresh[...] = (
        outer_beta * pout[...].astype(f32) + total / lax.axis_size("rep")
    ).astype(bf16)
    r_local = pltpu.make_async_copy(fresh, renewed.at[:, y_cols], p_sem.at[2])
    r_local.start()
    r_copies = []
    for i, d in enumerate(y_order):
        if d:
            c = remote(fresh, renewed.at[:, y_cols], r_sem, i, at_y(d))
            c.start()
            r_copies.append(c)

    outs = []

    def finish(ref, block, head):
        tri = spread(ref, upper, cross)
        full = tri + tri.T
        high = full.astype(bf16)
        low = (full - high.astype(f32)).astype(bf16)
        res = jnp.dot(
            jnp.concatenate([block, block], axis=1),
            jnp.concatenate([high, low], axis=0),
            preferred_element_type=f32,
        ).astype(bf16)
        j = len(outs)
        out[j] = res
        at = pl.multiple_of(head * HD, HD)
        c = pltpu.make_async_copy(out.at[j], update.at[0, :, pl.ds(at, HD)], out_sem.at[j])
        c.start()
        outs.append(c)

    def place(xo, d):
        return xo * nz + lax.rem(z + nz - d, nz)

    def my_block(k):
        return both[:rows, pl.ds(pl.multiple_of(k * HD, HD), HD)]

    def oth_block(k):
        return oth[:, pl.ds(pl.multiple_of(k * HD, HD), HD)]

    near = list(reversed(list(enumerate(z_order))))
    s_copies = {}
    fx_copies = {}

    def got_z(step):
        i, d = near[step]
        if d:
            m_copies[i].wait_recv()
        fx_copies[i] = remote(mz.at[i], mx.at[i], mx_sem, i, x_peer)
        fx_copies[i].start()
        s_copies[i] = remote(mz.at[i], ms.at[i], ms_sem, i, sibling)
        s_copies[i].start()
        k = place(xl, d)
        finish(mz.at[i], my_block(k), core * heads + k)

    def got_x(step):
        i, d = near[step]
        fx_copies[i].wait_recv()
        s_copies[nz + i] = remote(mx.at[i], ms.at[nz + i], ms_sem, nz + i, sibling)
        s_copies[nz + i].start()
        k = place(1 - xl, d)
        finish(mx.at[i], my_block(k), core * heads + k)

    def got_s(step, other):
        i, d = near[step]
        s_copies[other * nz + i].wait_recv()
        k = place(1 - xl if other else xl, d)
        finish(ms.at[other * nz + i], oth_block(k), (1 - core) * heads + k)

    for step in range(nz + 2):
        if step < nz:
            got_z(step)
        if 1 <= step <= nz:
            got_s(step - 1, 0)
            got_x(step - 1)
        if step >= 2:
            got_s(step - 2, 1)

    for c in core_copies + x_copies + list(y_copies.values()) + list(z_copies.values()) + [h_copy]:
        c.wait_send()
    for c in list(m_copies.values()) + list(fx_copies.values()) + list(s_copies.values()):
        c.wait_send()
    for c in r_copies:
        c.wait()
    r_local.wait()
    for c in outs:
        c.wait()


def shards(gradient, momentum, pseudo_gradient, outer_momentum):
    fsdp, rep = lax.axis_size("fsdp"), lax.axis_size("rep")
    nz, ny = fsdp // 4, rep // 2
    _, rows, features = gradient.shape
    cols = features // 2
    heads = cols // HD
    chunks = 4
    width = cols // chunks
    vmem = pltpu.VMEM
    dma = pltpu.SemaphoreType.DMA
    hbm = pl.BlockSpec(memory_space=pl.ANY)
    packs = vmem((nz, PACK, HD), f32)
    column = vmem((rows, HD), bf16)
    return pl.pallas_call(
        functools.partial(kernel, nz, ny),
        out_shape=(
            jax.ShapeDtypeStruct(gradient.shape, bf16),
            jax.ShapeDtypeStruct(outer_momentum.shape, bf16),
        ),
        in_specs=[hbm] * 4,
        out_specs=(hbm, hbm),
        scratch_shapes=[
            vmem((2 * chunks, rows, width), bf16),
            vmem((2 * chunks, rows, width), bf16),
            vmem((rows, cols), bf16),
            vmem((2 * rows, cols), bf16),
            packs, packs, packs, packs,
            vmem((8, HD), f32),
            packs, packs,
            vmem((2 * nz, PACK, HD), f32),
            vmem((2 * heads, rows, HD), bf16),
            vmem((ny, rows, HD), bf16),
            column, column, column, column, column,
            dma((2, 2 * chunks)),
            dma((2, chunks)),
            dma((2, nz)),
            dma((2, nz)),
            dma((2, nz)),
            dma((2, nz)),
            dma((2, 2 * nz)),
            dma((2 * heads,)),
            dma((2, ny)),
            dma((2, 1)),
            dma((2, ny)),
            dma((3,)),
        ],
        compiler_params=pltpu.CompilerParams(
            collective_id=0, has_side_effects=True, vmem_limit_bytes=48 * 1024 * 1024
        ),
    )(gradient, momentum, pseudo_gradient, outer_momentum)


def solution(mesh):
    return jax.shard_map(
        shards,
        mesh=mesh,
        in_specs=(
            P("rep", "fsdp", None),
            P("rep", "fsdp", None),
            P("rep", "fsdp", None),
            P("fsdp", None),
        ),
        out_specs=(P("rep", "fsdp", None), P("fsdp", None)),
        check_vma=False,
    )
```

```python
import functools
import math

import jax
import jax.numpy as jnp
from jax import lax
from jax.experimental import pallas as pl
from jax.experimental.pallas import tpu as pltpu
from jax.sharding import PartitionSpec as P

HD = 128
HALF = HD // 2
PACK = HALF + 8
ITERS = 5
DEPTH = 4

quint_a = 3.4445
quint_b = -4.775
quint_c = 2.0315
inner_beta = 0.95
outer_beta = 0.9
norm_eps = 1e-07
highest = lax.Precision.HIGHEST
f32 = jnp.float32
bf16 = jnp.bfloat16


def far_first(n):
    return sorted(range(n), key=lambda d: (-min(d, n - d), d))


def iota(axis, rows=HALF):
    return lax.broadcasted_iota(jnp.int32, (rows, HD), axis)


def masks():
    row, lane = iota(0), iota(1)
    upper = ((lane < HALF) & (lane >= row)) | ((lane >= HALF) & (lane - HALF < row))
    return upper, lane == row + HALF


def pack(full, upper, cross):
    top, low = full[:HALF], full[HALF:]
    diagonal = jnp.sum(jnp.where(cross, top, 0.0), axis=0, keepdims=True)
    return jnp.where(upper, top, low), jnp.broadcast_to(diagonal, (PACK - HALF, HD))


def spread(ref, upper, cross):
    body = ref[:HALF, :]
    top = jnp.where(upper, body, jnp.where(cross, ref[HALF : HALF + 1, :], 0.0))
    return jnp.concatenate([top, jnp.where(upper, 0.0, body)], axis=0)


def exact_dot(a, b):
    return jnp.dot(a, b, precision=highest, preferred_element_type=f32)


def kernel(
    nz, ny, grad, mom, pseudo, outer, update, renewed,
    gbuf, mbuf, oth, both, xs, xr, own, zr, mz, mx, ms, out,
    yr, pself, pout, half_own, half_in, fresh,
    in_sem, core_sem, x_sem, z_sem, mz_sem, mx_sem, ms_sem, out_sem, y_sem, h_sem, r_sem, p_sem,
):
    rep, fsdp = lax.axis_index("rep"), lax.axis_index("fsdp")
    core, xl, z = fsdp % 2, (fsdp // 2) % 2, fsdp // 4
    xh, y = rep % 2, rep // 2
    rows, cols = oth.shape
    heads = cols // HD
    z_order, y_order = far_first(nz), far_first(ny)

    def at_z(d):
        return {"fsdp": (lax.rem(z + d, nz) * 2 + xl) * 2 + core}

    def at_y(d):
        return {"rep": lax.rem(y + d, ny) * 2 + xh}

    x_peer = {"fsdp": (z * 2 + (1 - xl)) * 2 + core}
    sibling = {"fsdp": (z * 2 + xl) * 2 + (1 - core)}
    h_peer = {"rep": y * 2 + (1 - xh)}
    z_peers = [at_z(d) for d in range(1, nz)]
    y_peers = [at_y(d) for d in range(1, ny)]
    everyone = [sibling, x_peer, h_peer] + z_peers + y_peers

    barrier = pltpu.get_barrier_semaphore()
    for peer in everyone:
        pl.semaphore_signal(barrier, inc=1, device_id=peer, device_id_type=pl.DeviceIdType.MESH)

    def remote(src, dst, sems, i, peer):
        return pltpu.make_async_remote_copy(
            src_ref=src, dst_ref=dst, send_sem=sems.at[0, i], recv_sem=sems.at[1, i],
            device_id=peer, device_id_type=pl.DeviceIdType.MESH,
        )

    chunks = gbuf.shape[0] // 2
    width = gbuf.shape[2]
    loads = []
    for part in range(2):
        base = (1 - core if part == 0 else core) * cols
        for q in range(chunks):
            j = part * chunks + q
            where = pl.ds(pl.multiple_of(base + q * width, HD), width)
            pair = (
                pltpu.make_async_copy(grad.at[0, :, where], gbuf.at[j], in_sem.at[0, j]),
                pltpu.make_async_copy(mom.at[0, :, where], mbuf.at[j], in_sem.at[1, j]),
            )
            pair[0].start()
            pair[1].start()
            loads.append(pair)
    y_cols = pl.ds(pl.multiple_of(y * HD, HD), HD)
    self_copies = (
        pltpu.make_async_copy(pseudo.at[0, :, y_cols], pself, p_sem.at[0]),
        pltpu.make_async_copy(outer.at[:, y_cols], pout, p_sem.at[1]),
    )
    for c in self_copies:
        c.start()

    def nesterov(j):
        for c in loads[j]:
            c.wait()
        g = gbuf[j].astype(f32)
        return (g + inner_beta * (inner_beta * mbuf[j].astype(f32) + g)).astype(bf16)

    sends = []
    core_copies = []
    for q in range(chunks):
        here = pl.ds(q * width, width)
        oth[:, here] = nesterov(q)
        if q == 0:
            pl.semaphore_wait(barrier, len(everyone))
        c = remote(oth.at[:, here], both.at[pl.ds(rows, rows), here], core_sem, q, sibling)
        c.start()
        core_copies.append(c)
    for q in range(chunks):
        both[:rows, pl.ds(q * width, width)] = nesterov(chunks + q)
    y_copies = {}
    for i, d in enumerate(y_order):
        if d:
            there = pl.ds(pl.multiple_of(lax.rem(y + d, ny) * HD, HD), HD)
            c = remote(pseudo.at[0, :, there], yr.at[i], y_sem, i, at_y(d))
            c.start()
            y_copies[i] = c
    for c in core_copies:
        c.wait_recv()

    upper, cross = masks()

    def gram(xo, d):
        at = pl.multiple_of((xo * nz + lax.rem(z + d + nz, nz)) * HD, HD)
        block = both[:, pl.ds(at, HD)]
        full = lax.dot_general(block, block, (((0,), (0,)), ((), ())), preferred_element_type=f32)
        return pack(full, upper, cross)

    def replica_sum():
        for c in self_copies:
            c.wait()
        summed = pself[...].astype(f32)
        for i, c in y_copies.items():
            c.wait_recv()
            summed = summed + yr[i].astype(f32)
        half_own[...] = summed.astype(bf16)
        copy = remote(half_own, half_in, h_sem, 0, h_peer)
        copy.start()
        return copy

    def renew():
        h_copy.wait_recv()
        total = half_own[...].astype(f32) + half_in[...].astype(f32)
        fresh[...] = (
            outer_beta * pout[...].astype(f32) + total / lax.axis_size("rep")
        ).astype(bf16)
        copies = [pltpu.make_async_copy(fresh, renewed.at[:, y_cols], p_sem.at[2])]
        for i, d in enumerate(y_order):
            if d:
                copies.append(remote(fresh, renewed.at[:, y_cols], r_sem, i, at_y(d)))
        for c in copies:
            c.start()
        return copies

    x_copies = [remote(xs.at[i], xr.at[i], x_sem, i, x_peer) for i in range(nz)]
    for i, d in enumerate(z_order):
        xs[i, :HALF, :], xs[i, HALF:, :] = gram(1 - xl, d)
        if i < DEPTH:
            x_copies[i].start()
    for i, d in enumerate(z_order):
        own[i, :HALF, :], own[i, HALF:, :] = gram(xl, d)
    z_copies = []
    for i, d in enumerate(z_order[:-1]):
        x_copies[i].wait_recv()
        own[i] = own[i] + xr[i]
        z_copies.append(remote(own.at[i], zr.at[i], z_sem, i, at_z(d)))
        z_copies[i].start()
        if i + DEPTH < nz:
            x_copies[i].wait_send()
            x_copies[i + DEPTH].start()
        if i == (nz - 1) // 2:
            h_copy = replica_sum()

    r_copies = renew()
    last = nz - 1
    x_copies[last].wait_recv()
    own[last] = own[last] + xr[last]
    for i, c in enumerate(z_copies):
        c.wait_recv()
        own[last] = own[last] + zr[i]
    eye = iota(0, HD) == iota(1, HD)
    tri = spread(own.at[last], upper, cross)
    tri = jnp.where(eye, 0.5 * tri, tri)
    matrix = tri + tri.T
    square = 2.0 * jnp.sum(jnp.where(eye, tri, 0.0), keepdims=True)
    scale = 1.0 / (jnp.sqrt(square) + norm_eps)
    matrix = matrix * scale * scale
    ident = jnp.where(eye, quint_a, 0.0)
    product = None
    for sweep in range(ITERS):
        squared = exact_dot(matrix, matrix)
        poly = ident + quint_b * matrix + quint_c * squared
        product = poly if product is None else exact_dot(product, poly)
        if sweep < ITERS - 1:
            matrix = exact_dot(exact_dot(poly, matrix), poly)
    product = product * (scale * math.sqrt(rows * lax.axis_size("fsdp")))
    mz[0, :HALF, :], mz[0, HALF:, :] = pack(jnp.where(eye, 0.5 * product, product), upper, cross)

    outs = []

    def finish(ref, block, head):
        tri = spread(ref, upper, cross)
        full = tri + tri.T
        high = full.astype(bf16)
        low = (full - high.astype(f32)).astype(bf16)
        res = jnp.dot(
            jnp.concatenate([block, block], axis=1),
            jnp.concatenate([high, low], axis=0),
            preferred_element_type=f32,
        ).astype(bf16)
        j = len(outs)
        out[j] = res
        at = pl.multiple_of(head * HD, HD)
        c = pltpu.make_async_copy(out.at[j], update.at[0, :, pl.ds(at, HD)], out_sem.at[j])
        c.start()
        outs.append(c)

    def place(xo, slot):
        return xo * nz + lax.rem(z + nz - slot, nz)

    def my_block(k):
        return both[:rows, pl.ds(pl.multiple_of(k * HD, HD), HD)]

    def oth_block(k):
        return oth[:, pl.ds(pl.multiple_of(k * HD, HD), HD)]

    s_copies, fx_copies = {}, {}
    near = list(reversed(z_order))
    m_copies = {d: remote(mz.at[0], mz.at[d], mz_sem, d, at_z(d)) for d in near[1:]}

    def got_z(slot):
        if slot:
            m_copies[slot].wait_recv()
        fx_copies[slot] = remote(mz.at[slot], mx.at[slot], mx_sem, slot, x_peer)
        fx_copies[slot].start()
        s_copies[0, slot] = remote(mz.at[slot], ms.at[slot], ms_sem, slot, sibling)
        s_copies[0, slot].start()
        if slot == 0:
            for c in m_copies.values():
                c.start()
            for c in core_copies + x_copies[max(nz - DEPTH, 0) :] + list(y_copies.values()):
                c.wait_send()
            for c in z_copies + [h_copy]:
                c.wait_send()

    def got_x(slot):
        fx_copies[slot].wait_recv()
        s_copies[1, slot] = remote(mx.at[slot], ms.at[nz + slot], ms_sem, nz + slot, sibling)
        s_copies[1, slot].start()

    def got_s(other, slot):
        s_copies[other, slot].wait_recv()

    groups = [[0]] + [near[k : k + 2] for k in range(1, nz, 2)]
    for step in range(len(groups) + 2):
        fresh_z = groups[step] if step < len(groups) else []
        fresh_x = groups[step - 1] if 1 <= step <= len(groups) else []
        late_x = groups[step - 2] if step >= 2 else []
        for slot in fresh_z:
            got_z(slot)
        for slot in fresh_z:
            k = place(xl, slot)
            finish(mz.at[slot], my_block(k), core * heads + k)
        for slot in fresh_x:
            got_x(slot)
        for slot in fresh_x:
            k = place(1 - xl, slot)
            finish(mx.at[slot], my_block(k), core * heads + k)
        for slot in fresh_x:
            got_s(0, slot)
            k = place(xl, slot)
            finish(ms.at[slot], oth_block(k), (1 - core) * heads + k)
        for slot in late_x:
            got_s(1, slot)
            k = place(1 - xl, slot)
            finish(ms.at[nz + slot], oth_block(k), (1 - core) * heads + k)

    for group in (m_copies, fx_copies, s_copies):
        for c in group.values():
            c.wait_send()
    for c in r_copies + outs:
        c.wait()


def shards(gradient, momentum, pseudo_gradient, outer_momentum):
    fsdp, rep = lax.axis_size("fsdp"), lax.axis_size("rep")
    nz, ny = fsdp // 4, rep // 2
    _, rows, features = gradient.shape
    cols = features // 2
    heads = cols // HD
    chunks = 4
    width = cols // chunks
    vmem = pltpu.VMEM
    dma = pltpu.SemaphoreType.DMA
    hbm = pl.BlockSpec(memory_space=pl.ANY)
    packs = vmem((nz, PACK, HD), f32)
    column = vmem((rows, HD), bf16)
    return pl.pallas_call(
        functools.partial(kernel, nz, ny),
        out_shape=(
            jax.ShapeDtypeStruct(gradient.shape, bf16),
            jax.ShapeDtypeStruct(outer_momentum.shape, bf16),
        ),
        in_specs=[hbm] * 4,
        out_specs=(hbm, hbm),
        scratch_shapes=[
            vmem((2 * chunks, rows, width), bf16),
            vmem((2 * chunks, rows, width), bf16),
            vmem((rows, cols), bf16),
            vmem((2 * rows, cols), bf16),
            packs, packs, packs, packs, packs, packs,
            vmem((2 * nz, PACK, HD), f32),
            vmem((2 * heads, rows, HD), bf16),
            vmem((ny, rows, HD), bf16),
            column, column, column, column, column,
            dma((2, 2 * chunks)),
            dma((2, chunks)),
            dma((2, nz)),
            dma((2, nz)),
            dma((2, nz)),
            dma((2, nz)),
            dma((2, 2 * nz)),
            dma((2 * heads,)),
            dma((2, ny)),
            dma((2, 1)),
            dma((2, ny)),
            dma((3,)),
        ],
        compiler_params=pltpu.CompilerParams(
            collective_id=0, has_side_effects=True, vmem_limit_bytes=60 * 1024 * 1024
        ),
    )(gradient, momentum, pseudo_gradient, outer_momentum)


def solution(mesh):
    return jax.shard_map(
        shards,
        mesh=mesh,
        in_specs=(
            P("rep", "fsdp", None),
            P("rep", "fsdp", None),
            P("rep", "fsdp", None),
            P("fsdp", None),
        ),
        out_specs=(P("rep", "fsdp", None), P("fsdp", None)),
        check_vma=False,
    )
```

```python
import functools
import math

import jax
import jax.numpy as jnp
from jax import lax
from jax.experimental import pallas as pl
from jax.experimental.pallas import tpu as pltpu
from jax.sharding import PartitionSpec as P

HD = 128
HALF = HD // 2
PACK = HALF + 8
ITERS = 5
DEPTH = 4

quint_a = 3.4445
quint_b = -4.775
quint_c = 2.0315
inner_beta = 0.95
outer_beta = 0.9
norm_eps = 1e-07
highest = lax.Precision.HIGHEST
f32 = jnp.float32
bf16 = jnp.bfloat16


def far_first(n):
    return sorted(range(n), key=lambda d: (-min(d, n - d), d))


def iota(axis, rows=HALF):
    return lax.broadcasted_iota(jnp.int32, (rows, HD), axis)


def masks():
    row, lane = iota(0), iota(1)
    upper = ((lane < HALF) & (lane >= row)) | ((lane >= HALF) & (lane - HALF < row))
    return upper, lane == row + HALF


def pack(full, upper, cross):
    top, low = full[:HALF], full[HALF:]
    diagonal = jnp.sum(jnp.where(cross, top, 0.0), axis=0, keepdims=True)
    return jnp.where(upper, top, low), jnp.broadcast_to(diagonal, (PACK - HALF, HD))


def spread(ref, upper, cross):
    body = ref[:HALF, :]
    top = jnp.where(upper, body, jnp.where(cross, ref[HALF : HALF + 1, :], 0.0))
    return jnp.concatenate([top, jnp.where(upper, 0.0, body)], axis=0)


def exact_dot(a, b):
    return jnp.dot(a, b, precision=highest, preferred_element_type=f32)


def kernel(
    nz, ny, grad, mom, pseudo, outer, update, renewed,
    gbuf, mbuf, oth, both, xs, xr, own, zr, mz, mx, out,
    yr, pself, pout, half_own, half_in, fresh,
    in_sem, core_sem, x_sem, z_sem, mz_sem, mx_sem, os_sem, out_sem, y_sem, h_sem, r_sem, p_sem,
):
    rep, fsdp = lax.axis_index("rep"), lax.axis_index("fsdp")
    core, xl, z = fsdp % 2, (fsdp // 2) % 2, fsdp // 4
    xh, y = rep % 2, rep // 2
    rows, cols = oth.shape
    heads = cols // HD
    z_order, y_order = far_first(nz), far_first(ny)

    def at_z(d):
        return {"fsdp": (lax.rem(z + d, nz) * 2 + xl) * 2 + core}

    def at_y(d):
        return {"rep": lax.rem(y + d, ny) * 2 + xh}

    x_peer = {"fsdp": (z * 2 + (1 - xl)) * 2 + core}
    sibling = {"fsdp": (z * 2 + xl) * 2 + (1 - core)}
    h_peer = {"rep": y * 2 + (1 - xh)}
    z_peers = [at_z(d) for d in range(1, nz)]
    y_peers = [at_y(d) for d in range(1, ny)]
    everyone = [sibling, x_peer, h_peer] + z_peers + y_peers

    def remote(src, dst, sems, i, peer):
        return pltpu.make_async_remote_copy(
            src_ref=src, dst_ref=dst, send_sem=sems.at[0, i], recv_sem=sems.at[1, i],
            device_id=peer, device_id_type=pl.DeviceIdType.MESH,
        )

    chunks = gbuf.shape[0] // 2
    width = gbuf.shape[2]
    loads = []
    for part in range(2):
        base = (1 - core if part == 0 else core) * cols
        for q in range(chunks):
            j = part * chunks + q
            where = pl.ds(pl.multiple_of(base + q * width, HD), width)
            pair = (
                pltpu.make_async_copy(grad.at[0, :, where], gbuf.at[j], in_sem.at[0, j]),
                pltpu.make_async_copy(mom.at[0, :, where], mbuf.at[j], in_sem.at[1, j]),
            )
            if part == 0:
                pair[0].start()
                pair[1].start()
            loads.append(pair)
    barrier = pltpu.get_barrier_semaphore()
    for peer in everyone:
        pl.semaphore_signal(barrier, inc=1, device_id=peer, device_id_type=pl.DeviceIdType.MESH)
    y_cols = pl.ds(pl.multiple_of(y * HD, HD), HD)
    self_copies = (
        pltpu.make_async_copy(pseudo.at[0, :, y_cols], pself, p_sem.at[0]),
        pltpu.make_async_copy(outer.at[:, y_cols], pout, p_sem.at[1]),
    )

    def nesterov(j):
        for c in loads[j]:
            c.wait()
        g = gbuf[j].astype(f32)
        return (g + inner_beta * (inner_beta * mbuf[j].astype(f32) + g)).astype(bf16)

    core_copies = []
    for q in range(chunks):
        here = pl.ds(q * width, width)
        oth[:, here] = nesterov(q)
        if q == 0:
            for c in [c for pair in loads[chunks:] for c in pair] + list(self_copies):
                c.start()
            pl.semaphore_wait(barrier, len(everyone))
        c = remote(oth.at[:, here], both.at[pl.ds(rows, rows), here], core_sem, q, sibling)
        c.start()
        core_copies.append(c)
    for q in range(chunks):
        both[:rows, pl.ds(q * width, width)] = nesterov(chunks + q)
    y_copies = {}
    for i, d in enumerate(y_order):
        if d:
            there = pl.ds(pl.multiple_of(lax.rem(y + d, ny) * HD, HD), HD)
            c = remote(pseudo.at[0, :, there], yr.at[i], y_sem, i, at_y(d))
            c.start()
            y_copies[i] = c
    for c in core_copies:
        c.wait_recv()

    upper, cross = masks()

    def gram(xo, d):
        at = pl.multiple_of((xo * nz + lax.rem(z + d + nz, nz)) * HD, HD)
        block = both[:, pl.ds(at, HD)]
        full = lax.dot_general(block, block, (((0,), (0,)), ((), ())), preferred_element_type=f32)
        return pack(full, upper, cross)

    def replica_sum():
        for c in self_copies:
            c.wait()
        summed = pself[...].astype(f32)
        for i, c in y_copies.items():
            c.wait_recv()
            summed = summed + yr[i].astype(f32)
        half_own[...] = summed.astype(bf16)
        copy = remote(half_own, half_in, h_sem, 0, h_peer)
        copy.start()
        return copy

    def renew():
        h_copy.wait_recv()
        total = half_own[...].astype(f32) + half_in[...].astype(f32)
        fresh[...] = (
            outer_beta * pout[...].astype(f32) + total / lax.axis_size("rep")
        ).astype(bf16)
        copies = [pltpu.make_async_copy(fresh, renewed.at[:, y_cols], p_sem.at[2])]
        for i, d in enumerate(y_order):
            if d:
                copies.append(remote(fresh, renewed.at[:, y_cols], r_sem, i, at_y(d)))
        for c in copies:
            c.start()
        return copies

    x_copies = [remote(xs.at[i], xr.at[i], x_sem, i, x_peer) for i in range(nz)]
    for i, d in enumerate(z_order):
        xs[i, :HALF, :], xs[i, HALF:, :] = gram(1 - xl, d)
        if i < DEPTH:
            x_copies[i].start()
    for i, d in enumerate(z_order):
        own[i, :HALF, :], own[i, HALF:, :] = gram(xl, d)
    z_copies = []
    for i, d in enumerate(z_order[:-1]):
        x_copies[i].wait_recv()
        own[i] = own[i] + xr[i]
        z_copies.append(remote(own.at[i], zr.at[i], z_sem, i, at_z(d)))
        z_copies[i].start()
        if i + DEPTH < nz:
            x_copies[i].wait_send()
            x_copies[i + DEPTH].start()
        if i == (nz - 1) // 2:
            h_copy = replica_sum()

    r_copies = renew()
    last = nz - 1
    x_copies[last].wait_recv()
    own[last] = own[last] + xr[last]
    for i, c in enumerate(z_copies):
        c.wait_recv()
        own[last] = own[last] + zr[i]
    eye = iota(0, HD) == iota(1, HD)
    tri = spread(own.at[last], upper, cross)
    tri = jnp.where(eye, 0.5 * tri, tri)
    matrix = tri + tri.T
    square = 2.0 * jnp.sum(jnp.where(eye, tri, 0.0), keepdims=True)
    scale = 1.0 / (jnp.sqrt(square) + norm_eps)
    matrix = matrix * scale * scale
    ident = jnp.where(eye, quint_a, 0.0)
    product = None
    for sweep in range(ITERS):
        squared = exact_dot(matrix, matrix)
        poly = ident + quint_b * matrix + quint_c * squared
        product = poly if product is None else exact_dot(product, poly)
        if sweep < ITERS - 1:
            matrix = exact_dot(exact_dot(poly, matrix), poly)
    product = product * (scale * math.sqrt(rows * lax.axis_size("fsdp")))
    mz[0, :HALF, :], mz[0, HALF:, :] = pack(jnp.where(eye, 0.5 * product, product), upper, cross)

    outs = []

    def finish(ref, k):
        tri = spread(ref, upper, cross)
        full = tri + tri.T
        high = full.astype(bf16)
        low = (full - high.astype(f32)).astype(bf16)
        block = both[:, pl.ds(pl.multiple_of(k * HD, HD), HD)]
        j = len(outs)
        out[j] = jnp.dot(
            jnp.concatenate([block, block], axis=1),
            jnp.concatenate([high, low], axis=0),
            preferred_element_type=f32,
        ).astype(bf16)
        at = update.at[0, :, pl.ds(pl.multiple_of((core * heads + k) * HD, HD), HD)]
        pair = (
            remote(out.at[j, pl.ds(rows, rows)], at, os_sem, j, sibling),
            pltpu.make_async_copy(out.at[j, pl.ds(0, rows)], at, out_sem.at[j]),
        )
        for c in pair:
            c.start()
        outs.append(pair)

    def place(xo, slot):
        return xo * nz + lax.rem(z + nz - slot, nz)

    fx_copies = {}
    near = list(reversed(z_order))
    m_copies = {d: remote(mz.at[0], mz.at[d], mz_sem, d, at_z(d)) for d in near[1:]}

    def got_z(slot):
        if slot:
            m_copies[slot].wait_recv()
        fx_copies[slot] = remote(mz.at[slot], mx.at[slot], mx_sem, slot, x_peer)
        fx_copies[slot].start()
        if slot == 0:
            for c in m_copies.values():
                c.start()
            for c in core_copies + x_copies[max(nz - DEPTH, 0) :] + list(y_copies.values()):
                c.wait_send()
            for c in z_copies + [h_copy]:
                c.wait_send()

    groups = [[0]] + [near[k : k + 2] for k in range(1, nz, 2)]
    for step in range(len(groups) + 1):
        fresh_z = groups[step] if step < len(groups) else []
        fresh_x = groups[step - 1] if step else []
        for slot in fresh_z:
            got_z(slot)
        for slot in fresh_z:
            finish(mz.at[slot], place(xl, slot))
        for slot in fresh_x:
            fx_copies[slot].wait_recv()
        for slot in fresh_x:
            finish(mx.at[slot], place(1 - xl, slot))

    for group in (m_copies, fx_copies):
        for c in group.values():
            c.wait_send()
    for c in r_copies:
        c.wait()
    for pair in outs:
        for c in pair:
            c.wait()


def shards(gradient, momentum, pseudo_gradient, outer_momentum):
    fsdp, rep = lax.axis_size("fsdp"), lax.axis_size("rep")
    nz, ny = fsdp // 4, rep // 2
    _, rows, features = gradient.shape
    cols = features // 2
    heads = cols // HD
    chunks = 4
    width = cols // chunks
    vmem = pltpu.VMEM
    dma = pltpu.SemaphoreType.DMA
    anywhere = pl.BlockSpec(memory_space=pl.ANY)
    packs = vmem((nz, PACK, HD), f32)
    column = vmem((rows, HD), bf16)
    return pl.pallas_call(
        functools.partial(kernel, nz, ny),
        out_shape=(
            jax.ShapeDtypeStruct(gradient.shape, bf16),
            jax.ShapeDtypeStruct(outer_momentum.shape, bf16),
        ),
        in_specs=[pl.BlockSpec(memory_space=pltpu.HBM)] * 4,
        out_specs=(anywhere, anywhere),
        scratch_shapes=[
            vmem((2 * chunks, rows, width), bf16),
            vmem((2 * chunks, rows, width), bf16),
            vmem((rows, cols), bf16),
            vmem((2 * rows, cols), bf16),
            packs, packs, packs, packs, packs, packs,
            vmem((heads, 2 * rows, HD), bf16),
            vmem((ny, rows, HD), bf16),
            column, column, column, column, column,
            dma((2, 2 * chunks)),
            dma((2, chunks)),
            dma((2, nz)),
            dma((2, nz)),
            dma((2, nz)),
            dma((2, nz)),
            dma((2, heads)),
            dma((heads,)),
            dma((2, ny)),
            dma((2, 1)),
            dma((2, ny)),
            dma((3,)),
        ],
        compiler_params=pltpu.CompilerParams(
            collective_id=0, has_side_effects=True, vmem_limit_bytes=60 * 1024 * 1024
        ),
    )(gradient, momentum, pseudo_gradient, outer_momentum)


def solution(mesh):
    return jax.shard_map(
        shards,
        mesh=mesh,
        in_specs=(
            P("rep", "fsdp", None),
            P("rep", "fsdp", None),
            P("rep", "fsdp", None),
            P("fsdp", None),
        ),
        out_specs=(P("rep", "fsdp", None), P("fsdp", None)),
        check_vma=False,
    )
```

```python
import functools
import math

import jax
import jax.numpy as jnp
from jax import lax
from jax.experimental import pallas as pl
from jax.experimental.pallas import tpu as pltpu
from jax.sharding import PartitionSpec as P

HD = 128
HALF = HD // 2
PACK = HALF + 8
ITERS = 5

quint_a = 3.4445
quint_b = -4.775
quint_c = 2.0315
inner_beta = 0.95
outer_beta = 0.9
norm_eps = 1e-07
highest = lax.Precision.HIGHEST
f32 = jnp.float32
bf16 = jnp.bfloat16


def far_first(n):
    return sorted(range(n), key=lambda d: (-min(d, n - d), d))


def iota(axis, rows=HALF):
    return lax.broadcasted_iota(jnp.int32, (rows, HD), axis)


def masks():
    row, lane = iota(0), iota(1)
    upper = ((lane < HALF) & (lane >= row)) | ((lane >= HALF) & (lane - HALF < row))
    return upper, lane == row + HALF


def pack(full, upper, cross):
    top, low = full[:HALF], full[HALF:]
    diagonal = jnp.sum(jnp.where(cross, top, 0.0), axis=0, keepdims=True)
    return jnp.where(upper, top, low), jnp.broadcast_to(diagonal, (PACK - HALF, HD))


def spread(ref, upper, cross):
    body = ref[:HALF, :]
    top = jnp.where(upper, body, jnp.where(cross, ref[HALF : HALF + 1, :], 0.0))
    return jnp.concatenate([top, jnp.where(upper, 0.0, body)], axis=0)


def exact_dot(a, b):
    return jnp.dot(a, b, precision=highest, preferred_element_type=f32)


def kernel(
    nz, ny, grad, mom, pseudo, outer, update, renewed,
    gbuf, mbuf, oth, both, xs, xr, own, zr, mz, mx, out,
    yr, pself, pout, half_own, half_in, fresh,
    in_sem, core_sem, x_sem, z_sem, mz_sem, mx_sem, os_sem, out_sem, y_sem, h_sem, r_sem, p_sem,
):
    rep, fsdp = lax.axis_index("rep"), lax.axis_index("fsdp")
    core, xl, z = fsdp % 2, (fsdp // 2) % 2, fsdp // 4
    xh, y = rep % 2, rep // 2
    rows, cols = oth.shape
    heads = cols // HD
    z_order, y_order = far_first(nz), far_first(ny)

    def at_z(d):
        return {"fsdp": (lax.rem(z + d, nz) * 2 + xl) * 2 + core}

    def at_y(d):
        return {"rep": lax.rem(y + d, ny) * 2 + xh}

    x_peer = {"fsdp": (z * 2 + (1 - xl)) * 2 + core}
    sibling = {"fsdp": (z * 2 + xl) * 2 + (1 - core)}
    h_peer = {"rep": y * 2 + (1 - xh)}
    z_peers = [at_z(d) for d in range(1, nz)]
    y_peers = [at_y(d) for d in range(1, ny)]
    everyone = [sibling, x_peer, h_peer] + z_peers + y_peers

    def remote(src, dst, sems, i, peer):
        return pltpu.make_async_remote_copy(
            src_ref=src, dst_ref=dst, send_sem=sems.at[0, i], recv_sem=sems.at[1, i],
            device_id=peer, device_id_type=pl.DeviceIdType.MESH,
        )

    chunks = gbuf.shape[0] // 2
    width = gbuf.shape[2]
    loads = []
    for part in range(2):
        base = (1 - core if part == 0 else core) * cols
        for q in range(chunks):
            j = part * chunks + q
            where = pl.ds(pl.multiple_of(base + q * width, HD), width)
            pair = (
                pltpu.make_async_copy(grad.at[0, :, where], gbuf.at[j], in_sem.at[0, j]),
                pltpu.make_async_copy(mom.at[0, :, where], mbuf.at[j], in_sem.at[1, j]),
            )
            if part == 0:
                pair[0].start()
                pair[1].start()
            loads.append(pair)
    barrier = pltpu.get_barrier_semaphore()
    for peer in everyone:
        pl.semaphore_signal(barrier, inc=1, device_id=peer, device_id_type=pl.DeviceIdType.MESH)
    y_cols = pl.ds(pl.multiple_of(y * HD, HD), HD)
    self_copies = (
        pltpu.make_async_copy(pseudo.at[0, :, y_cols], pself, p_sem.at[0]),
        pltpu.make_async_copy(outer.at[:, y_cols], pout, p_sem.at[1]),
    )

    def nesterov(j):
        for c in loads[j]:
            c.wait()
        g = gbuf[j].astype(f32)
        return (g + inner_beta * (inner_beta * mbuf[j].astype(f32) + g)).astype(bf16)

    core_copies = []
    for q in range(chunks):
        here = pl.ds(q * width, width)
        oth[:, here] = nesterov(q)
        if q == 0:
            for c in [c for pair in loads[chunks:] for c in pair] + list(self_copies):
                c.start()
            pl.semaphore_wait(barrier, len(everyone))
        c = remote(oth.at[:, here], both.at[pl.ds(rows, rows), here], core_sem, q, sibling)
        c.start()
        core_copies.append(c)
    for q in range(chunks):
        both[:rows, pl.ds(q * width, width)] = nesterov(chunks + q)
    y_copies = {}
    for i, d in enumerate(y_order):
        if d:
            there = pl.ds(pl.multiple_of(lax.rem(y + d, ny) * HD, HD), HD)
            c = remote(pseudo.at[0, :, there], yr.at[i], y_sem, i, at_y(d))
            c.start()
            y_copies[i] = c
    for c in core_copies:
        c.wait_recv()

    upper, cross = masks()

    def gram(xo, d):
        at = pl.multiple_of((xo * nz + lax.rem(z + d + nz, nz)) * HD, HD)
        block = both[:, pl.ds(at, HD)]
        full = lax.dot_general(block, block, (((0,), (0,)), ((), ())), preferred_element_type=f32)
        return pack(full, upper, cross)

    def replica_sum():
        for c in self_copies:
            c.wait()
        summed = pself[...].astype(f32)
        for i, c in y_copies.items():
            c.wait_recv()
            summed = summed + yr[i].astype(f32)
        half_own[...] = summed.astype(bf16)
        copy = remote(half_own, half_in, h_sem, 0, h_peer)
        copy.start()
        return copy

    def renew():
        h_copy.wait_recv()
        total = half_own[...].astype(f32) + half_in[...].astype(f32)
        fresh[...] = (
            outer_beta * pout[...].astype(f32) + total / lax.axis_size("rep")
        ).astype(bf16)
        copies = [pltpu.make_async_copy(fresh, renewed.at[:, y_cols], p_sem.at[2])]
        for i, d in enumerate(y_order):
            if d:
                copies.append(remote(fresh, renewed.at[:, y_cols], r_sem, i, at_y(d)))
        for c in copies:
            c.start()
        return copies

    last = nz - 1
    z_copies = {}
    for half, xo, mine, theirs in ((0, 1 - xl, xs, xr), (1, xl, own, zr)):
        for i, d in enumerate(z_order):
            mine[i, :HALF, :], mine[i, HALF:, :] = gram(xo, d)
            if d:
                slot = half * nz + i
                z_copies[half, i] = remote(mine.at[i], theirs.at[i], z_sem, slot, at_z(d))
                z_copies[half, i].start()

    def z_sum(half, mine, theirs):
        total = mine[last]
        for i in range(last):
            z_copies[half, i].wait_recv()
            total = total + theirs[i]
        mine[last] = total

    z_sum(0, xs, xr)
    x_copy = remote(xs.at[last], xr.at[last], x_sem, 0, x_peer)
    x_copy.start()
    h_copy = replica_sum()
    z_sum(1, own, zr)
    x_copy.wait_recv()
    own[last] = own[last] + xr[last]

    eye = iota(0, HD) == iota(1, HD)
    tri = spread(own.at[last], upper, cross)
    tri = jnp.where(eye, 0.5 * tri, tri)
    matrix = tri + tri.T
    square = 2.0 * jnp.sum(jnp.where(eye, tri, 0.0), keepdims=True)
    scale = 1.0 / (jnp.sqrt(square) + norm_eps)
    matrix = matrix * scale * scale
    ident = jnp.where(eye, quint_a, 0.0)
    product = None
    for sweep in range(ITERS):
        squared = exact_dot(matrix, matrix)
        poly = ident + quint_b * matrix + quint_c * squared
        product = poly if product is None else exact_dot(product, poly)
        if sweep < ITERS - 1:
            matrix = exact_dot(exact_dot(poly, matrix), poly)
    product = product * (scale * math.sqrt(rows * lax.axis_size("fsdp")))
    mz[0, :HALF, :], mz[0, HALF:, :] = pack(jnp.where(eye, 0.5 * product, product), upper, cross)

    outs = []

    def finish(ref, k):
        tri = spread(ref, upper, cross)
        full = tri + tri.T
        high = full.astype(bf16)
        low = (full - high.astype(f32)).astype(bf16)
        block = both[:, pl.ds(pl.multiple_of(k * HD, HD), HD)]
        j = len(outs)
        out[j] = jnp.dot(
            jnp.concatenate([block, block], axis=1),
            jnp.concatenate([high, low], axis=0),
            preferred_element_type=f32,
        ).astype(bf16)
        at = update.at[0, :, pl.ds(pl.multiple_of((core * heads + k) * HD, HD), HD)]
        pair = (
            remote(out.at[j, pl.ds(rows, rows)], at, os_sem, j, sibling),
            pltpu.make_async_copy(out.at[j, pl.ds(0, rows)], at, out_sem.at[j]),
        )
        for c in pair:
            c.start()
        outs.append(pair)

    def place(xo, slot):
        return xo * nz + lax.rem(z + nz - slot, nz)

    fx_copy = remote(mz.at[0], mx.at[0], mx_sem, 0, x_peer)
    fx_copy.start()
    m_copies = {}
    for half, blocks, sems in ((0, mz, mz_sem), (1, mx, mx_sem)):
        if half:
            r_copies = renew()
            finish(mz.at[0], place(xl, 0))
            fx_copy.wait_recv()
        for d in z_order[:-1]:
            m_copies[half, d] = remote(blocks.at[0], blocks.at[d], sems, d, at_z(d))
            m_copies[half, d].start()
    finish(mx.at[0], place(1 - xl, 0))
    for c in core_copies + list(y_copies.values()) + list(z_copies.values()):
        c.wait_send()
    for c in (x_copy, h_copy, fx_copy):
        c.wait_send()

    near = list(reversed(z_order))
    for half, blocks, xo in ((0, mz, xl), (1, mx, 1 - xl)):
        for k in range(1, nz, 2):
            for slot in near[k : k + 2]:
                m_copies[half, slot].wait_recv()
            for slot in near[k : k + 2]:
                finish(blocks.at[slot], place(xo, slot))

    for c in m_copies.values():
        c.wait_send()
    for c in r_copies:
        c.wait()
    for pair in outs:
        for c in pair:
            c.wait()


def shards(gradient, momentum, pseudo_gradient, outer_momentum):
    fsdp, rep = lax.axis_size("fsdp"), lax.axis_size("rep")
    nz, ny = fsdp // 4, rep // 2
    _, rows, features = gradient.shape
    cols = features // 2
    heads = cols // HD
    chunks = 4
    width = cols // chunks
    vmem = pltpu.VMEM
    dma = pltpu.SemaphoreType.DMA
    anywhere = pl.BlockSpec(memory_space=pl.ANY)
    packs = vmem((nz, PACK, HD), f32)
    column = vmem((rows, HD), bf16)
    return pl.pallas_call(
        functools.partial(kernel, nz, ny),
        out_shape=(
            jax.ShapeDtypeStruct(gradient.shape, bf16),
            jax.ShapeDtypeStruct(outer_momentum.shape, bf16),
        ),
        in_specs=[pl.BlockSpec(memory_space=pltpu.HBM)] * 4,
        out_specs=(anywhere, anywhere),
        scratch_shapes=[
            vmem((2 * chunks, rows, width), bf16),
            vmem((2 * chunks, rows, width), bf16),
            vmem((rows, cols), bf16),
            vmem((2 * rows, cols), bf16),
            packs, packs, packs, packs, packs, packs,
            vmem((heads, 2 * rows, HD), bf16),
            vmem((ny, rows, HD), bf16),
            column, column, column, column, column,
            dma((2, 2 * chunks)),
            dma((2, chunks)),
            dma((2, 1)),
            dma((2, 2 * nz)),
            dma((2, nz)),
            dma((2, nz)),
            dma((2, heads)),
            dma((heads,)),
            dma((2, ny)),
            dma((2, 1)),
            dma((2, ny)),
            dma((3,)),
        ],
        compiler_params=pltpu.CompilerParams(
            collective_id=0, has_side_effects=True, vmem_limit_bytes=60 * 1024 * 1024
        ),
    )(gradient, momentum, pseudo_gradient, outer_momentum)


def solution(mesh):
    return jax.shard_map(
        shards,
        mesh=mesh,
        in_specs=(
            P("rep", "fsdp", None),
            P("rep", "fsdp", None),
            P("rep", "fsdp", None),
            P("fsdp", None),
        ),
        out_specs=(P("rep", "fsdp", None), P("fsdp", None)),
        check_vma=False,
    )
```

```python
import functools
import math

import jax
import jax.numpy as jnp
from jax import lax
from jax.experimental import pallas as pl
from jax.experimental.pallas import tpu as pltpu
from jax.sharding import PartitionSpec as P

HD = 128
HALF = HD // 2
PACK = HALF + 8
ITERS = 5
DEPTH = 4

quint_a = 3.4445
quint_b = -4.775
quint_c = 2.0315
inner_beta = 0.95
outer_beta = 0.9
norm_eps = 1e-07
highest = lax.Precision.HIGHEST
f32 = jnp.float32
bf16 = jnp.bfloat16


def far_first(n):
    return sorted(range(n), key=lambda d: (-min(d, n - d), d))


def iota(axis, rows=HALF):
    return lax.broadcasted_iota(jnp.int32, (rows, HD), axis)


def masks():
    row, lane = iota(0), iota(1)
    upper = ((lane < HALF) & (lane >= row)) | ((lane >= HALF) & (lane - HALF < row))
    return upper, lane == row + HALF


def pack(full, upper, cross):
    top, low = full[:HALF], full[HALF:]
    diagonal = jnp.sum(jnp.where(cross, top, 0.0), axis=0, keepdims=True)
    return jnp.where(upper, top, low), jnp.broadcast_to(diagonal, (PACK - HALF, HD))


def spread(ref, upper, cross):
    body = ref[:HALF, :]
    top = jnp.where(upper, body, jnp.where(cross, ref[HALF : HALF + 1, :], 0.0))
    return jnp.concatenate([top, jnp.where(upper, 0.0, body)], axis=0)


def exact_dot(a, b):
    return jnp.dot(a, b, precision=highest, preferred_element_type=f32)


def kernel(
    nz, ny, grad, mom, pseudo, outer, update, renewed,
    gbuf, mbuf, oth, both, xs, xr, own, zr, mz, mx, out,
    yr, pself, pout, half_own, half_in, fresh,
    in_sem, core_sem, x_sem, z_sem, mz_sem, mx_sem, os_sem, out_sem, y_sem, h_sem, r_sem, p_sem,
):
    rep, fsdp = lax.axis_index("rep"), lax.axis_index("fsdp")
    core, xl, z = fsdp % 2, (fsdp // 2) % 2, fsdp // 4
    xh, y = rep % 2, rep // 2
    rows, cols = oth.shape
    heads = cols // HD
    z_order, y_order = far_first(nz), far_first(ny)

    def at_z(d):
        return {"fsdp": (lax.rem(z + d, nz) * 2 + xl) * 2 + core}

    def at_y(d):
        return {"rep": lax.rem(y + d, ny) * 2 + xh}

    x_peer = {"fsdp": (z * 2 + (1 - xl)) * 2 + core}
    sibling = {"fsdp": (z * 2 + xl) * 2 + (1 - core)}
    h_peer = {"rep": y * 2 + (1 - xh)}
    z_peers = [at_z(d) for d in range(1, nz)]
    y_peers = [at_y(d) for d in range(1, ny)]
    everyone = [sibling, x_peer, h_peer] + z_peers + y_peers

    def remote(src, dst, sems, i, peer):
        return pltpu.make_async_remote_copy(
            src_ref=src, dst_ref=dst, send_sem=sems.at[0, i], recv_sem=sems.at[1, i],
            device_id=peer, device_id_type=pl.DeviceIdType.MESH,
        )

    chunks = gbuf.shape[0] // 2
    width = gbuf.shape[2]
    loads = []
    for part in range(2):
        base = (1 - core if part == 0 else core) * cols
        for q in range(chunks):
            j = part * chunks + q
            where = pl.ds(pl.multiple_of(base + q * width, HD), width)
            pair = (
                pltpu.make_async_copy(grad.at[0, :, where], gbuf.at[j], in_sem.at[0, j]),
                pltpu.make_async_copy(mom.at[0, :, where], mbuf.at[j], in_sem.at[1, j]),
            )
            if part == 0:
                pair[0].start()
                pair[1].start()
            loads.append(pair)
    barrier = pltpu.get_barrier_semaphore()
    for peer in everyone:
        pl.semaphore_signal(barrier, inc=1, device_id=peer, device_id_type=pl.DeviceIdType.MESH)
    y_cols = pl.ds(pl.multiple_of(y * HD, HD), HD)
    self_copies = (
        pltpu.make_async_copy(pseudo.at[0, :, y_cols], pself, p_sem.at[0]),
        pltpu.make_async_copy(outer.at[:, y_cols], pout, p_sem.at[1]),
    )

    def nesterov(j):
        for c in loads[j]:
            c.wait()
        g = gbuf[j].astype(f32)
        return (g + inner_beta * (inner_beta * mbuf[j].astype(f32) + g)).astype(bf16)

    core_copies = []
    for q in range(chunks):
        here = pl.ds(q * width, width)
        oth[:, here] = nesterov(q)
        if q == 0:
            for c in [c for pair in loads[chunks:] for c in pair] + list(self_copies):
                c.start()
            pl.semaphore_wait(barrier, len(everyone))
        c = remote(oth.at[:, here], both.at[pl.ds(rows, rows), here], core_sem, q, sibling)
        c.start()
        core_copies.append(c)
    for q in range(chunks):
        both[:rows, pl.ds(q * width, width)] = nesterov(chunks + q)
    y_copies = {}
    for i, d in enumerate(y_order):
        if d:
            there = pl.ds(pl.multiple_of(lax.rem(y + d, ny) * HD, HD), HD)
            c = remote(pseudo.at[0, :, there], yr.at[i], y_sem, i, at_y(d))
            c.start()
            y_copies[i] = c
    for c in core_copies:
        c.wait_recv()

    upper, cross = masks()

    def gram(xo, d):
        at = pl.multiple_of((xo * nz + lax.rem(z + d + nz, nz)) * HD, HD)
        block = both[:, pl.ds(at, HD)]
        full = lax.dot_general(block, block, (((0,), (0,)), ((), ())), preferred_element_type=f32)
        return pack(full, upper, cross)

    def replica_sum():
        for c in self_copies:
            c.wait()
        summed = pself[...].astype(f32)
        for i, c in y_copies.items():
            c.wait_recv()
            summed = summed + yr[i].astype(f32)
        half_own[...] = summed.astype(bf16)
        copy = remote(half_own, half_in, h_sem, 0, h_peer)
        copy.start()
        return copy

    def renew():
        h_copy.wait_recv()
        total = half_own[...].astype(f32) + half_in[...].astype(f32)
        fresh[...] = (
            outer_beta * pout[...].astype(f32) + total / lax.axis_size("rep")
        ).astype(bf16)
        copies = [pltpu.make_async_copy(fresh, renewed.at[:, y_cols], p_sem.at[2])]
        for i, d in enumerate(y_order):
            if d:
                copies.append(remote(fresh, renewed.at[:, y_cols], r_sem, i, at_y(d)))
        for c in copies:
            c.start()
        return copies

    x_copies = [remote(xs.at[i], xr.at[i], x_sem, i, x_peer) for i in range(nz)]
    for i, d in enumerate(z_order):
        xs[i, :HALF, :], xs[i, HALF:, :] = gram(1 - xl, d)
        if i < DEPTH:
            x_copies[i].start()
    for i, d in enumerate(z_order):
        own[i, :HALF, :], own[i, HALF:, :] = gram(xl, d)
    z_copies = []
    for i, d in enumerate(z_order[:-1]):
        x_copies[i].wait_recv()
        own[i] = own[i] + xr[i]
        z_copies.append(remote(own.at[i], zr.at[i], z_sem, i, at_z(d)))
        z_copies[i].start()
        if i + DEPTH < nz:
            x_copies[i].wait_send()
            x_copies[i + DEPTH].start()

    h_copy = replica_sum()

    last = nz - 1
    x_copies[last].wait_recv()
    own[last] = own[last] + xr[last]
    for i, c in enumerate(z_copies):
        c.wait_recv()
        own[last] = own[last] + zr[i]
    eye = iota(0, HD) == iota(1, HD)
    tri = spread(own.at[last], upper, cross)
    tri = jnp.where(eye, 0.5 * tri, tri)
    matrix = tri + tri.T
    square = 2.0 * jnp.sum(jnp.where(eye, tri, 0.0), keepdims=True)
    scale = 1.0 / (jnp.sqrt(square) + norm_eps)
    matrix = matrix * scale * scale
    ident = jnp.where(eye, quint_a, 0.0)
    product = None
    for sweep in range(ITERS):
        squared = exact_dot(matrix, matrix)
        poly = ident + quint_b * matrix + quint_c * squared
        product = poly if product is None else exact_dot(product, poly)
        if sweep < ITERS - 1:
            matrix = exact_dot(exact_dot(poly, matrix), poly)
    product = product * (scale * math.sqrt(rows * lax.axis_size("fsdp")))
    mz[0, :HALF, :], mz[0, HALF:, :] = pack(jnp.where(eye, 0.5 * product, product), upper, cross)

    outs = []

    def finish(ref, k):
        tri = spread(ref, upper, cross)
        full = tri + tri.T
        high = full.astype(bf16)
        low = (full - high.astype(f32)).astype(bf16)
        block = both[:, pl.ds(pl.multiple_of(k * HD, HD), HD)]
        j = len(outs)
        out[j] = jnp.dot(
            jnp.concatenate([block, block], axis=1),
            jnp.concatenate([high, low], axis=0),
            preferred_element_type=f32,
        ).astype(bf16)
        at = update.at[0, :, pl.ds(pl.multiple_of((core * heads + k) * HD, HD), HD)]
        pair = (
            remote(out.at[j, pl.ds(rows, rows)], at, os_sem, j, sibling),
            pltpu.make_async_copy(out.at[j, pl.ds(0, rows)], at, out_sem.at[j]),
        )
        for c in pair:
            c.start()
        outs.append(pair)

    def place(xo, slot):
        return xo * nz + lax.rem(z + nz - slot, nz)

    fx_copies, r_copies = {}, []
    near = list(reversed(z_order))
    m_copies = {d: remote(mz.at[0], mz.at[d], mz_sem, d, at_z(d)) for d in near[1:]}

    def got_z(slot):
        if slot:
            m_copies[slot].wait_recv()
        fx_copies[slot] = remote(mz.at[slot], mx.at[slot], mx_sem, slot, x_peer)
        fx_copies[slot].start()
        if slot == 0:
            for c in m_copies.values():
                c.start()
            for c in core_copies + x_copies[max(nz - DEPTH, 0) :] + list(y_copies.values()):
                c.wait_send()
            for c in z_copies + [h_copy]:
                c.wait_send()
            r_copies.extend(renew())

    groups = [[0]] + [near[k : k + 2] for k in range(1, nz, 2)]
    for group in groups:
        for slot in group:
            got_z(slot)
        for slot in group:
            finish(mz.at[slot], place(xl, slot))
    for group in groups:
        for slot in group:
            fx_copies[slot].wait_recv()
        for slot in group:
            finish(mx.at[slot], place(1 - xl, slot))

    for group in (m_copies, fx_copies):
        for c in group.values():
            c.wait_send()
    for c in r_copies:
        c.wait()
    for pair in outs:
        for c in pair:
            c.wait()


def shards(gradient, momentum, pseudo_gradient, outer_momentum):
    fsdp, rep = lax.axis_size("fsdp"), lax.axis_size("rep")
    nz, ny = fsdp // 4, rep // 2
    _, rows, features = gradient.shape
    cols = features // 2
    heads = cols // HD
    chunks = 4
    width = cols // chunks
    vmem = pltpu.VMEM
    dma = pltpu.SemaphoreType.DMA
    anywhere = pl.BlockSpec(memory_space=pl.ANY)
    packs = vmem((nz, PACK, HD), f32)
    column = vmem((rows, HD), bf16)
    return pl.pallas_call(
        functools.partial(kernel, nz, ny),
        out_shape=(
            jax.ShapeDtypeStruct(gradient.shape, bf16),
            jax.ShapeDtypeStruct(outer_momentum.shape, bf16),
        ),
        in_specs=[pl.BlockSpec(memory_space=pltpu.HBM)] * 4,
        out_specs=(anywhere, anywhere),
        scratch_shapes=[
            vmem((2 * chunks, rows, width), bf16),
            vmem((2 * chunks, rows, width), bf16),
            vmem((rows, cols), bf16),
            vmem((2 * rows, cols), bf16),
            packs, packs, packs, packs, packs, packs,
            vmem((heads, 2 * rows, HD), bf16),
            vmem((ny, rows, HD), bf16),
            column, column, column, column, column,
            dma((2, 2 * chunks)),
            dma((2, chunks)),
            dma((2, nz)),
            dma((2, nz)),
            dma((2, nz)),
            dma((2, nz)),
            dma((2, heads)),
            dma((heads,)),
            dma((2, ny)),
            dma((2, 1)),
            dma((2, ny)),
            dma((3,)),
        ],
        compiler_params=pltpu.CompilerParams(
            collective_id=0, has_side_effects=True, vmem_limit_bytes=60 * 1024 * 1024
        ),
    )(gradient, momentum, pseudo_gradient, outer_momentum)


def solution(mesh):
    return jax.shard_map(
        shards,
        mesh=mesh,
        in_specs=(
            P("rep", "fsdp", None),
            P("rep", "fsdp", None),
            P("rep", "fsdp", None),
            P("fsdp", None),
        ),
        out_specs=(P("rep", "fsdp", None), P("fsdp", None)),
        check_vma=False,
    )
```

```python
import functools
import math

import jax
import jax.numpy as jnp
from jax import lax
from jax.experimental import pallas as pl
from jax.experimental.pallas import tpu as pltpu
from jax.sharding import PartitionSpec as P

HD = 128
HALF = HD // 2
PACK = HALF + 8
ITERS = 5
DEPTH = 4

quint_a = 3.4445
quint_b = -4.775
quint_c = 2.0315
inner_beta = 0.95
outer_beta = 0.9
norm_eps = 1e-07
highest = lax.Precision.HIGHEST
f32 = jnp.float32
bf16 = jnp.bfloat16


def far_first(n):
    return sorted(range(n), key=lambda d: (-min(d, n - d), d))


def iota(axis, rows=HALF):
    return lax.broadcasted_iota(jnp.int32, (rows, HD), axis)


def masks():
    row, lane = iota(0), iota(1)
    upper = ((lane < HALF) & (lane >= row)) | ((lane >= HALF) & (lane - HALF < row))
    return upper, lane == row + HALF


def pack(full, upper, cross):
    top, low = full[:HALF], full[HALF:]
    diagonal = jnp.sum(jnp.where(cross, top, 0.0), axis=0, keepdims=True)
    return jnp.where(upper, top, low), jnp.broadcast_to(diagonal, (PACK - HALF, HD))


def spread(ref, upper, cross):
    body = ref[:HALF, :]
    top = jnp.where(upper, body, jnp.where(cross, ref[HALF : HALF + 1, :], 0.0))
    return jnp.concatenate([top, jnp.where(upper, 0.0, body)], axis=0)


def exact_dot(a, b):
    return jnp.dot(a, b, precision=highest, preferred_element_type=f32)


def kernel(
    nz, ny, grad, mom, pseudo, outer, update, renewed,
    gbuf, mbuf, oth, both, xs, xr, own, zr, mz, mx, out,
    yr, pself, pout, half_own, half_in, fresh,
    in_sem, core_sem, x_sem, z_sem, mz_sem, mx_sem, os_sem, out_sem, y_sem, h_sem, r_sem, p_sem,
):
    rep, fsdp = lax.axis_index("rep"), lax.axis_index("fsdp")
    core, xl, z = fsdp % 2, (fsdp // 2) % 2, fsdp // 4
    xh, y = rep % 2, rep // 2
    rows, cols = oth.shape
    heads = cols // HD
    z_order, y_order = far_first(nz), far_first(ny)

    def at_z(d):
        return {"fsdp": (lax.rem(z + d, nz) * 2 + xl) * 2 + core}

    def at_y(d):
        return {"rep": lax.rem(y + d, ny) * 2 + xh}

    x_peer = {"fsdp": (z * 2 + (1 - xl)) * 2 + core}
    sibling = {"fsdp": (z * 2 + xl) * 2 + (1 - core)}
    h_peer = {"rep": y * 2 + (1 - xh)}
    z_peers = [at_z(d) for d in range(1, nz)]
    y_peers = [at_y(d) for d in range(1, ny)]
    everyone = [sibling, x_peer, h_peer] + z_peers + y_peers

    def remote(src, dst, sems, i, peer):
        return pltpu.make_async_remote_copy(
            src_ref=src, dst_ref=dst, send_sem=sems.at[0, i], recv_sem=sems.at[1, i],
            device_id=peer, device_id_type=pl.DeviceIdType.MESH,
        )

    chunks = gbuf.shape[0] // 2
    width = gbuf.shape[2]
    loads = []
    for part in range(2):
        base = (1 - core if part == 0 else core) * cols
        for q in range(chunks):
            j = part * chunks + q
            where = pl.ds(pl.multiple_of(base + q * width, HD), width)
            pair = (
                pltpu.make_async_copy(grad.at[0, :, where], gbuf.at[j], in_sem.at[0, j]),
                pltpu.make_async_copy(mom.at[0, :, where], mbuf.at[j], in_sem.at[1, j]),
            )
            if part == 0:
                pair[0].start()
                pair[1].start()
            loads.append(pair)
    barrier = pltpu.get_barrier_semaphore()
    for peer in everyone:
        pl.semaphore_signal(barrier, inc=1, device_id=peer, device_id_type=pl.DeviceIdType.MESH)
    y_cols = pl.ds(pl.multiple_of(y * HD, HD), HD)
    self_copies = (
        pltpu.make_async_copy(pseudo.at[0, :, y_cols], pself, p_sem.at[0]),
        pltpu.make_async_copy(outer.at[:, y_cols], pout, p_sem.at[1]),
    )

    def nesterov(j):
        for c in loads[j]:
            c.wait()
        g = gbuf[j].astype(f32)
        return (g + inner_beta * (inner_beta * mbuf[j].astype(f32) + g)).astype(bf16)

    core_copies = []
    for q in range(chunks):
        here = pl.ds(q * width, width)
        oth[:, here] = nesterov(q)
        if q == 0:
            for c in [c for pair in loads[chunks:] for c in pair] + list(self_copies):
                c.start()
            pl.semaphore_wait(barrier, len(everyone))
        c = remote(oth.at[:, here], both.at[pl.ds(rows, rows), here], core_sem, q, sibling)
        c.start()
        core_copies.append(c)
    for q in range(chunks):
        both[:rows, pl.ds(q * width, width)] = nesterov(chunks + q)
    y_copies = {}
    for i, d in enumerate(y_order):
        if d:
            there = pl.ds(pl.multiple_of(lax.rem(y + d, ny) * HD, HD), HD)
            c = remote(pseudo.at[0, :, there], yr.at[i], y_sem, i, at_y(d))
            c.start()
            y_copies[i] = c
    for c in core_copies:
        c.wait_recv()

    upper, cross = masks()

    def gram(xo, d):
        at = pl.multiple_of((xo * nz + lax.rem(z + d + nz, nz)) * HD, HD)
        block = both[:, pl.ds(at, HD)]
        full = lax.dot_general(block, block, (((0,), (0,)), ((), ())), preferred_element_type=f32)
        return pack(full, upper, cross)

    def replica_sum():
        for c in self_copies:
            c.wait()
        summed = pself[...].astype(f32)
        for i, c in y_copies.items():
            c.wait_recv()
            summed = summed + yr[i].astype(f32)
        half_own[...] = summed.astype(bf16)
        copy = remote(half_own, half_in, h_sem, 0, h_peer)
        copy.start()
        return copy

    def renew():
        h_copy.wait_recv()
        total = half_own[...].astype(f32) + half_in[...].astype(f32)
        fresh[...] = (
            outer_beta * pout[...].astype(f32) + total / lax.axis_size("rep")
        ).astype(bf16)
        copies = [pltpu.make_async_copy(fresh, renewed.at[:, y_cols], p_sem.at[2])]
        for i, d in enumerate(y_order):
            if d:
                copies.append(remote(fresh, renewed.at[:, y_cols], r_sem, i, at_y(d)))
        for c in copies:
            c.start()
        return copies

    x_copies = [remote(xs.at[i], xr.at[i], x_sem, i, x_peer) for i in range(nz)]
    for i, d in enumerate(z_order):
        xs[i, :HALF, :], xs[i, HALF:, :] = gram(1 - xl, d)
        if i < DEPTH:
            x_copies[i].start()
    for i, d in enumerate(z_order):
        own[i, :HALF, :], own[i, HALF:, :] = gram(xl, d)
    z_copies = []
    for i, d in enumerate(z_order[:-1]):
        x_copies[i].wait_recv()
        own[i] = own[i] + xr[i]
        z_copies.append(remote(own.at[i], zr.at[i], z_sem, i, at_z(d)))
        z_copies[i].start()
        if i + DEPTH < nz:
            x_copies[i].wait_send()
            x_copies[i + DEPTH].start()

    h_copy = replica_sum()

    last = nz - 1
    x_copies[last].wait_recv()
    own[last] = own[last] + xr[last]
    for i, c in enumerate(z_copies):
        c.wait_recv()
        own[last] = own[last] + zr[i]
    eye = iota(0, HD) == iota(1, HD)
    tri = spread(own.at[last], upper, cross)
    tri = jnp.where(eye, 0.5 * tri, tri)
    matrix = tri + tri.T
    square = 2.0 * jnp.sum(jnp.where(eye, tri, 0.0), keepdims=True)
    scale = 1.0 / (jnp.sqrt(square) + norm_eps)
    matrix = matrix * scale * scale
    ident = jnp.where(eye, quint_a, 0.0)
    product = None
    for sweep in range(ITERS):
        squared = exact_dot(matrix, matrix)
        poly = ident + quint_b * matrix + quint_c * squared
        product = poly if product is None else exact_dot(product, poly)
        if sweep < ITERS - 1:
            matrix = exact_dot(exact_dot(poly, matrix), poly)
    product = product * (scale * math.sqrt(rows * lax.axis_size("fsdp")))
    mz[0, :HALF, :], mz[0, HALF:, :] = pack(jnp.where(eye, 0.5 * product, product), upper, cross)

    outs = []

    def finish(ref, k):
        tri = spread(ref, upper, cross)
        full = tri + tri.T
        high = full.astype(bf16)
        low = (full - high.astype(f32)).astype(bf16)
        block = both[:, pl.ds(pl.multiple_of(k * HD, HD), HD)]
        j = len(outs)
        out[j] = jnp.dot(
            jnp.concatenate([block, block], axis=1),
            jnp.concatenate([high, low], axis=0),
            preferred_element_type=f32,
        ).astype(bf16)
        at = update.at[0, :, pl.ds(pl.multiple_of((core * heads + k) * HD, HD), HD)]
        pair = (
            remote(out.at[j, pl.ds(rows, rows)], at, os_sem, j, sibling),
            pltpu.make_async_copy(out.at[j, pl.ds(0, rows)], at, out_sem.at[j]),
        )
        for c in pair:
            c.start()
        outs.append(pair)

    def place(xo, slot):
        return xo * nz + lax.rem(z + nz - slot, nz)

    fx_copies, r_copies = {}, []
    near = list(reversed(z_order))
    m_copies = {d: remote(mz.at[0], mz.at[d], mz_sem, d, at_z(d)) for d in z_order[:-1]}

    def got_z(slot):
        if slot:
            m_copies[slot].wait_recv()
        fx_copies[slot] = remote(mz.at[slot], mx.at[slot], mx_sem, slot, x_peer)
        fx_copies[slot].start()
        if slot == 0:
            for c in m_copies.values():
                c.start()
            for c in core_copies + x_copies[max(nz - DEPTH, 0) :] + list(y_copies.values()):
                c.wait_send()
            for c in z_copies + [h_copy]:
                c.wait_send()
            r_copies.extend(renew())

    groups = [[0]] + [near[k : k + 2] for k in range(1, nz, 2)]
    for group in groups:
        for slot in group:
            got_z(slot)
        for slot in group:
            finish(mz.at[slot], place(xl, slot))
    for group in groups:
        for slot in group:
            fx_copies[slot].wait_recv()
        for slot in group:
            finish(mx.at[slot], place(1 - xl, slot))

    for group in (m_copies, fx_copies):
        for c in group.values():
            c.wait_send()
    for c in r_copies:
        c.wait()
    for pair in outs:
        for c in pair:
            c.wait()


def shards(gradient, momentum, pseudo_gradient, outer_momentum):
    fsdp, rep = lax.axis_size("fsdp"), lax.axis_size("rep")
    nz, ny = fsdp // 4, rep // 2
    _, rows, features = gradient.shape
    cols = features // 2
    heads = cols // HD
    chunks = 4
    width = cols // chunks
    vmem = pltpu.VMEM
    dma = pltpu.SemaphoreType.DMA
    anywhere = pl.BlockSpec(memory_space=pl.ANY)
    packs = vmem((nz, PACK, HD), f32)
    column = vmem((rows, HD), bf16)
    return pl.pallas_call(
        functools.partial(kernel, nz, ny),
        out_shape=(
            jax.ShapeDtypeStruct(gradient.shape, bf16),
            jax.ShapeDtypeStruct(outer_momentum.shape, bf16),
        ),
        in_specs=[pl.BlockSpec(memory_space=pltpu.HBM)] * 4,
        out_specs=(anywhere, anywhere),
        scratch_shapes=[
            vmem((2 * chunks, rows, width), bf16),
            vmem((2 * chunks, rows, width), bf16),
            vmem((rows, cols), bf16),
            vmem((2 * rows, cols), bf16),
            packs, packs, packs, packs, packs, packs,
            vmem((heads, 2 * rows, HD), bf16),
            vmem((ny, rows, HD), bf16),
            column, column, column, column, column,
            dma((2, 2 * chunks)),
            dma((2, chunks)),
            dma((2, nz)),
            dma((2, nz)),
            dma((2, nz)),
            dma((2, nz)),
            dma((2, heads)),
            dma((heads,)),
            dma((2, ny)),
            dma((2, 1)),
            dma((2, ny)),
            dma((3,)),
        ],
        compiler_params=pltpu.CompilerParams(
            collective_id=0, has_side_effects=True, vmem_limit_bytes=60 * 1024 * 1024
        ),
    )(gradient, momentum, pseudo_gradient, outer_momentum)


def solution(mesh):
    return jax.shard_map(
        shards,
        mesh=mesh,
        in_specs=(
            P("rep", "fsdp", None),
            P("rep", "fsdp", None),
            P("rep", "fsdp", None),
            P("fsdp", None),
        ),
        out_specs=(P("rep", "fsdp", None), P("fsdp", None)),
        check_vma=False,
    )
```

```python
import functools
import math

import jax
import jax.numpy as jnp
from jax import lax
from jax.experimental import pallas as pl
from jax.experimental.pallas import tpu as pltpu
from jax.sharding import PartitionSpec as P

HD = 128
HALF = HD // 2
PACK = HALF + 8
ITERS = 5
DEPTH = 8

quint_a = 3.4445
quint_b = -4.775
quint_c = 2.0315
inner_beta = 0.95
outer_beta = 0.9
norm_eps = 1e-07
highest = lax.Precision.HIGHEST
f32 = jnp.float32
bf16 = jnp.bfloat16


def far_first(n):
    return sorted(range(n), key=lambda d: (-min(d, n - d), d))


def iota(axis, rows=HALF):
    return lax.broadcasted_iota(jnp.int32, (rows, HD), axis)


def masks():
    row, lane = iota(0), iota(1)
    upper = ((lane < HALF) & (lane >= row)) | ((lane >= HALF) & (lane - HALF < row))
    return upper, lane == row + HALF


def pack(full, upper, cross):
    top, low = full[:HALF], full[HALF:]
    diagonal = jnp.sum(jnp.where(cross, top, 0.0), axis=0, keepdims=True)
    return jnp.where(upper, top, low), jnp.broadcast_to(diagonal, (PACK - HALF, HD))


def spread(ref, upper, cross):
    body = ref[:HALF, :]
    top = jnp.where(upper, body, jnp.where(cross, ref[HALF : HALF + 1, :], 0.0))
    return jnp.concatenate([top, jnp.where(upper, 0.0, body)], axis=0)


def exact_dot(a, b):
    return jnp.dot(a, b, precision=highest, preferred_element_type=f32)


def kernel(
    nz, ny, grad, mom, pseudo, outer, update, renewed,
    gbuf, mbuf, oth, both, xs, xr, own, zr, mz, mx, out,
    yr, pself, pout, half_own, half_in, fresh,
    in_sem, core_sem, x_sem, z_sem, mz_sem, mx_sem, os_sem, out_sem, y_sem, h_sem, r_sem, p_sem,
):
    rep, fsdp = lax.axis_index("rep"), lax.axis_index("fsdp")
    core, xl, z = fsdp % 2, (fsdp // 2) % 2, fsdp // 4
    xh, y = rep % 2, rep // 2
    rows, cols = oth.shape
    heads = cols // HD
    z_order, y_order = far_first(nz), far_first(ny)

    def at_z(d):
        return {"fsdp": (lax.rem(z + d, nz) * 2 + xl) * 2 + core}

    def at_y(d):
        return {"rep": lax.rem(y + d, ny) * 2 + xh}

    x_peer = {"fsdp": (z * 2 + (1 - xl)) * 2 + core}
    sibling = {"fsdp": (z * 2 + xl) * 2 + (1 - core)}
    h_peer = {"rep": y * 2 + (1 - xh)}
    z_peers = [at_z(d) for d in range(1, nz)]
    y_peers = [at_y(d) for d in range(1, ny)]
    everyone = [sibling, x_peer, h_peer] + z_peers + y_peers

    def remote(src, dst, sems, i, peer):
        return pltpu.make_async_remote_copy(
            src_ref=src, dst_ref=dst, send_sem=sems.at[0, i], recv_sem=sems.at[1, i],
            device_id=peer, device_id_type=pl.DeviceIdType.MESH,
        )

    chunks = gbuf.shape[0] // 2
    width = gbuf.shape[2]
    loads = []
    for part in range(2):
        base = (1 - core if part == 0 else core) * cols
        for q in range(chunks):
            j = part * chunks + q
            where = pl.ds(pl.multiple_of(base + q * width, HD), width)
            pair = (
                pltpu.make_async_copy(grad.at[0, :, where], gbuf.at[j], in_sem.at[0, j]),
                pltpu.make_async_copy(mom.at[0, :, where], mbuf.at[j], in_sem.at[1, j]),
            )
            if part == 0:
                pair[0].start()
                pair[1].start()
            loads.append(pair)
    barrier = pltpu.get_barrier_semaphore()
    for peer in everyone:
        pl.semaphore_signal(barrier, inc=1, device_id=peer, device_id_type=pl.DeviceIdType.MESH)
    y_cols = pl.ds(pl.multiple_of(y * HD, HD), HD)
    self_copies = (
        pltpu.make_async_copy(pseudo.at[0, :, y_cols], pself, p_sem.at[0]),
        pltpu.make_async_copy(outer.at[:, y_cols], pout, p_sem.at[1]),
    )

    def nesterov(j):
        for c in loads[j]:
            c.wait()
        g = gbuf[j].astype(f32)
        return (g + inner_beta * (inner_beta * mbuf[j].astype(f32) + g)).astype(bf16)

    core_copies = []
    for q in range(chunks):
        here = pl.ds(q * width, width)
        oth[:, here] = nesterov(q)
        if q == 0:
            for c in [c for pair in loads[chunks:] for c in pair] + list(self_copies):
                c.start()
            pl.semaphore_wait(barrier, len(everyone))
        c = remote(oth.at[:, here], both.at[pl.ds(rows, rows), here], core_sem, q, sibling)
        c.start()
        core_copies.append(c)
    for q in range(chunks):
        both[:rows, pl.ds(q * width, width)] = nesterov(chunks + q)
    y_copies = {}
    for i, d in enumerate(y_order):
        if d:
            there = pl.ds(pl.multiple_of(lax.rem(y + d, ny) * HD, HD), HD)
            c = remote(pseudo.at[0, :, there], yr.at[i], y_sem, i, at_y(d))
            c.start()
            y_copies[i] = c
    for c in core_copies:
        c.wait_recv()

    upper, cross = masks()

    def gram(xo, d):
        at = pl.multiple_of((xo * nz + lax.rem(z + d + nz, nz)) * HD, HD)
        block = both[:, pl.ds(at, HD)]
        full = lax.dot_general(block, block, (((0,), (0,)), ((), ())), preferred_element_type=f32)
        return pack(full, upper, cross)

    def replica_sum():
        for c in self_copies:
            c.wait()
        summed = pself[...].astype(f32)
        for i, c in y_copies.items():
            c.wait_recv()
            summed = summed + yr[i].astype(f32)
        half_own[...] = summed.astype(bf16)
        copy = remote(half_own, half_in, h_sem, 0, h_peer)
        copy.start()
        return copy

    def renew():
        h_copy.wait_recv()
        total = half_own[...].astype(f32) + half_in[...].astype(f32)
        fresh[...] = (
            outer_beta * pout[...].astype(f32) + total / lax.axis_size("rep")
        ).astype(bf16)
        copies = [pltpu.make_async_copy(fresh, renewed.at[:, y_cols], p_sem.at[2])]
        for i, d in enumerate(y_order):
            if d:
                copies.append(remote(fresh, renewed.at[:, y_cols], r_sem, i, at_y(d)))
        for c in copies:
            c.start()
        return copies

    x_copies = [remote(xs.at[i], xr.at[i], x_sem, i, x_peer) for i in range(nz)]
    for i, d in enumerate(z_order):
        xs[i, :HALF, :], xs[i, HALF:, :] = gram(1 - xl, d)
        if i < DEPTH:
            x_copies[i].start()
    for i, d in enumerate(z_order):
        own[i, :HALF, :], own[i, HALF:, :] = gram(xl, d)
    z_copies = []
    for i, d in enumerate(z_order[:-1]):
        x_copies[i].wait_recv()
        own[i] = own[i] + xr[i]
        z_copies.append(remote(own.at[i], zr.at[i], z_sem, i, at_z(d)))
        z_copies[i].start()
        if i + DEPTH < nz:
            x_copies[i].wait_send()
            x_copies[i + DEPTH].start()

    h_copy = replica_sum()

    last = nz - 1
    x_copies[last].wait_recv()
    own[last] = own[last] + xr[last]
    for i, c in enumerate(z_copies):
        c.wait_recv()
        own[last] = own[last] + zr[i]
    eye = iota(0, HD) == iota(1, HD)
    tri = spread(own.at[last], upper, cross)
    tri = jnp.where(eye, 0.5 * tri, tri)
    matrix = tri + tri.T
    square = 2.0 * jnp.sum(jnp.where(eye, tri, 0.0), keepdims=True)
    scale = 1.0 / (jnp.sqrt(square) + norm_eps)
    matrix = matrix * scale * scale
    ident = jnp.where(eye, quint_a, 0.0)
    product = None
    for sweep in range(ITERS):
        squared = exact_dot(matrix, matrix)
        poly = ident + quint_b * matrix + quint_c * squared
        product = poly if product is None else exact_dot(product, poly)
        if sweep < ITERS - 1:
            matrix = exact_dot(exact_dot(poly, matrix), poly)
    product = product * (scale * math.sqrt(rows * lax.axis_size("fsdp")))
    mz[0, :HALF, :], mz[0, HALF:, :] = pack(jnp.where(eye, 0.5 * product, product), upper, cross)

    outs = []

    def finish(ref, k):
        tri = spread(ref, upper, cross)
        full = tri + tri.T
        high = full.astype(bf16)
        low = (full - high.astype(f32)).astype(bf16)
        block = both[:, pl.ds(pl.multiple_of(k * HD, HD), HD)]
        j = len(outs)
        out[j] = jnp.dot(
            jnp.concatenate([block, block], axis=1),
            jnp.concatenate([high, low], axis=0),
            preferred_element_type=f32,
        ).astype(bf16)
        at = update.at[0, :, pl.ds(pl.multiple_of((core * heads + k) * HD, HD), HD)]
        pair = (
            remote(out.at[j, pl.ds(rows, rows)], at, os_sem, j, sibling),
            pltpu.make_async_copy(out.at[j, pl.ds(0, rows)], at, out_sem.at[j]),
        )
        for c in pair:
            c.start()
        outs.append(pair)

    def place(xo, slot):
        return xo * nz + lax.rem(z + nz - slot, nz)

    fx_copies, r_copies = {}, []
    near = list(reversed(z_order))
    m_copies = {d: remote(mz.at[0], mz.at[d], mz_sem, d, at_z(d)) for d in near[1:]}

    def got_z(slot):
        if slot:
            m_copies[slot].wait_recv()
        fx_copies[slot] = remote(mz.at[slot], mx.at[slot], mx_sem, slot, x_peer)
        fx_copies[slot].start()
        if slot == 0:
            for c in m_copies.values():
                c.start()
            for c in core_copies + x_copies[max(nz - DEPTH, 0) :] + list(y_copies.values()):
                c.wait_send()
            for c in z_copies + [h_copy]:
                c.wait_send()
            r_copies.extend(renew())

    groups = [[0]] + [near[k : k + 2] for k in range(1, nz, 2)]
    for group in groups:
        for slot in group:
            got_z(slot)
        for slot in group:
            finish(mz.at[slot], place(xl, slot))
    for group in groups:
        for slot in group:
            fx_copies[slot].wait_recv()
        for slot in group:
            finish(mx.at[slot], place(1 - xl, slot))

    for group in (m_copies, fx_copies):
        for c in group.values():
            c.wait_send()
    for c in r_copies:
        c.wait()
    for pair in outs:
        for c in pair:
            c.wait()


def shards(gradient, momentum, pseudo_gradient, outer_momentum):
    fsdp, rep = lax.axis_size("fsdp"), lax.axis_size("rep")
    nz, ny = fsdp // 4, rep // 2
    _, rows, features = gradient.shape
    cols = features // 2
    heads = cols // HD
    chunks = 4
    width = cols // chunks
    vmem = pltpu.VMEM
    dma = pltpu.SemaphoreType.DMA
    anywhere = pl.BlockSpec(memory_space=pl.ANY)
    packs = vmem((nz, PACK, HD), f32)
    column = vmem((rows, HD), bf16)
    return pl.pallas_call(
        functools.partial(kernel, nz, ny),
        out_shape=(
            jax.ShapeDtypeStruct(gradient.shape, bf16),
            jax.ShapeDtypeStruct(outer_momentum.shape, bf16),
        ),
        in_specs=[pl.BlockSpec(memory_space=pltpu.HBM)] * 4,
        out_specs=(anywhere, anywhere),
        scratch_shapes=[
            vmem((2 * chunks, rows, width), bf16),
            vmem((2 * chunks, rows, width), bf16),
            vmem((rows, cols), bf16),
            vmem((2 * rows, cols), bf16),
            packs, packs, packs, packs, packs, packs,
            vmem((heads, 2 * rows, HD), bf16),
            vmem((ny, rows, HD), bf16),
            column, column, column, column, column,
            dma((2, 2 * chunks)),
            dma((2, chunks)),
            dma((2, nz)),
            dma((2, nz)),
            dma((2, nz)),
            dma((2, nz)),
            dma((2, heads)),
            dma((heads,)),
            dma((2, ny)),
            dma((2, 1)),
            dma((2, ny)),
            dma((3,)),
        ],
        compiler_params=pltpu.CompilerParams(
            collective_id=0, has_side_effects=True, vmem_limit_bytes=60 * 1024 * 1024
        ),
    )(gradient, momentum, pseudo_gradient, outer_momentum)


def solution(mesh):
    return jax.shard_map(
        shards,
        mesh=mesh,
        in_specs=(
            P("rep", "fsdp", None),
            P("rep", "fsdp", None),
            P("rep", "fsdp", None),
            P("fsdp", None),
        ),
        out_specs=(P("rep", "fsdp", None), P("fsdp", None)),
        check_vma=False,
    )
```
